256 devices in a mesh: dp: 32 (over y, z), tensor: 8 (over x, core).
Axes of the slice: x: 4, y: 4, z: 8, core: 2. Of those that a mesh axis runs over, the one named last changes fastest.
Arguments:
- attn_in: bfloat16 [64, 1024, 4096], P('dp', None, 'tensor'), may hold values from -6 to 6
- v_grad: bfloat16 [64, 1024, 1024], P('dp', None, 'tensor'), may hold values from -6 to 6
- mlp_hidden: bfloat16 [64, 1024, 14336], P('dp', None, 'tensor'), may hold values from -6 to 6
- out_grad: bfloat16 [64, 1024, 4096], P('dp', None, 'tensor'), may hold values from -6 to 6
- proj_in_attn: bfloat16 [64, 4096], P(None, 'tensor'), may hold values from -0.09375 to 0.09375
- proj_out_value: bfloat16 [64, 1024], P(None, 'tensor'), may hold values from -0.1875 to 0.1875
- proj_in_mlp: bfloat16 [64, 14336], P(None, 'tensor'), may hold values from -0.046875 to 0.046875
- proj_out_mlp: bfloat16 [64, 4096], P(None, 'tensor'), may hold values from -0.09375 to 0.09375
- query_features: bfloat16 [2, 1024, 4096], P(None, 'tensor', 'dp'), may hold values from -0.0625 to 0.0625
Outputs:
- fisher: float32 [4096, 2, 4096], P('dp', None, 'tensor')
- scores: float32 [64, 1024], P('dp', 'tensor')
The draws below stay inside these ranges and needn't reach their ends.
All inputs are finite; a program needn't handle non-finite values.
Results may differ from the reference program's by a relative error of at most 0.0055.
The reference program's roundings to bfloat16 on the way (of `features`) count: a program that leaves them out, or rounds other values in their place, can miss the bound.
Values may be sent and summed in bfloat16 or wider, within the bound.
No kernel may reach another device: no remote copies, remote signals or barrier semaphores. Data moves between devices by JAX's collectives and lax.ppermute only.
A program may use at most 128 MiB of HBM per device.

```python
import math
import jax
import jax.numpy as jnp
from jax import lax

D = 4096
DKV = 1024
FF = 14336
RANK = 64
PROJ = 2
SEQ = 1024
FEAT = 4096
EXAMPLES = 64
NQ = 1024


def level_of(stream_key, extent, pieces, low, largest):
    level, own = 1.0, jax.random.fold_in(stream_key, 6)
    for dim, parts in pieces:
        heights = jnp.exp(jax.random.uniform(jax.random.fold_in(own, dim), (parts,), jnp.float32, low / len(pieces), largest / len(pieces)))
        level = level * jnp.repeat(heights, extent[dim] // parts).reshape([-1 if axis == dim else 1 for axis in range(len(extent))])
    return level


def centred(own_key, extent, spread, bound, pieces=(), held_as=jnp.bfloat16):
    loudness = level_of(own_key, extent, pieces, -0.22, 0.18) if pieces else 1.0
    values = jax.random.normal(own_key, extent, jnp.float32) * spread * loudness
    return jnp.minimum(jnp.maximum(values, -bound), bound).astype(held_as)


def setup_inputs(seed: int = 0) -> dict:
    streams_of = jax.random.split(jax.random.key(seed), 10)
    attn_in = centred(streams_of[0], (EXAMPLES, SEQ, D), 1.0, 6.0, ((0, 32), (2, 8)))
    v_grad = centred(streams_of[1], (EXAMPLES, SEQ, DKV), 1.0, 6.0, ((0, 32), (2, 8)))
    mlp_hidden = centred(streams_of[2], (EXAMPLES, SEQ, FF), 1.0, 6.0, ((0, 32), (2, 8)))
    out_grad = centred(streams_of[3], (EXAMPLES, SEQ, D), 1.0, 6.0, ((0, 32), (2, 8)))
    proj_in_attn = centred(streams_of[4], (RANK, D), D ** -0.5, 0.09375, ((1, 8),))
    proj_out_value = centred(streams_of[5], (RANK, DKV), DKV ** -0.5, 0.1875, ((1, 8),))
    proj_in_mlp = centred(streams_of[6], (RANK, FF), FF ** -0.5, 0.046875, ((1, 8),))
    proj_out_mlp = centred(streams_of[7], (RANK, D), D ** -0.5, 0.09375, ((1, 8),))
    query_features = centred(streams_of[8], (PROJ, NQ, FEAT), (PROJ * FEAT) ** -0.5, 0.0625, ((1, 8), (2, 32)))
    return dict(attn_in=attn_in, v_grad=v_grad, mlp_hidden=mlp_hidden, out_grad=out_grad, proj_in_attn=proj_in_attn, proj_out_value=proj_out_value, proj_in_mlp=proj_in_mlp, proj_out_mlp=proj_out_mlp, query_features=query_features)


def reference(attn_in, v_grad, mlp_hidden, out_grad, proj_in_attn, proj_out_value, proj_in_mlp, proj_out_mlp, query_features):
    scale_factor = 1.0 / math.sqrt(SEQ)

    def one_sequence(inputs):
        attn_rows, value_rows, hidden_rows, output_rows = inputs
        value_out = jnp.dot(value_rows, proj_out_value.T, preferred_element_type=jnp.float32).astype(jnp.bfloat16)
        value_in = jnp.dot(attn_rows, proj_in_attn.T, preferred_element_type=jnp.float32).astype(jnp.bfloat16)
        down_out = jnp.dot(output_rows, proj_out_mlp.T, preferred_element_type=jnp.float32).astype(jnp.bfloat16)
        down_in = jnp.dot(hidden_rows, proj_in_mlp.T, preferred_element_type=jnp.float32).astype(jnp.bfloat16)
        value_part = jnp.dot(value_out.T, value_in, preferred_element_type=jnp.float32) * scale_factor
        down_part = jnp.dot(down_out.T, down_in, preferred_element_type=jnp.float32) * scale_factor
        stacked = jnp.stack([value_part.reshape(-1), down_part.reshape(-1)], axis=0)
        return stacked.astype(jnp.bfloat16)
    features = lax.map(one_sequence, (attn_in, v_grad, mlp_hidden, out_grad))
    widened = features.astype(jnp.float32)
    gram_sums = jnp.einsum('epf,epg->fpg', widened, widened, precision=lax.Precision.HIGHEST)
    damping = 0.5 * lax.optimization_barrier(jnp.sum(widened * widened, axis=(0, 2))) / (EXAMPLES * FEAT)
    identity_mask = jnp.eye(FEAT, dtype=jnp.float32)[:, None, :]
    fisher = gram_sums / EXAMPLES + damping[None, :, None] * identity_mask
    norm_scale = jnp.sqrt(lax.optimization_barrier(jnp.mean(widened * widened, axis=(1, 2))) + 1e-06)
    raw_scores = jnp.einsum('epf,pqf->eq', widened, query_features.astype(jnp.float32), precision=lax.Precision.HIGHEST)
    scores = raw_scores / norm_scale[:, None]
    return (fisher, scores)
```

```python
import functools
import math

import jax
import jax.numpy as jnp
from jax import lax
from jax.experimental import pallas as pl
from jax.experimental.pallas import tpu as pltpu
from jax.sharding import PartitionSpec as P

F32 = jnp.float32
BF16 = jnp.bfloat16
LANES = 128
VMEM = pltpu.VMEM
NT = (((1,), (1,)), ((), ()))
TN = (((0,), (0,)), ((), ()))


def dot(a, b, dims):
    return lax.dot_general(a, b, dims, preferred_element_type=F32)


def project_kernel(place, v_ref, a_ref, g_ref, m_ref, wv_ref, wa_ref, wg_ref, wm_ref, out_ref):
    sequence, block = pl.program_id(0), pl.program_id(1)
    tokens = v_ref.shape[1]
    rank = wv_ref.shape[0]
    rows = pl.ds(pl.multiple_of(block * tokens, tokens), tokens)
    first = lax.rem(2 * sequence + 4 - place[0], 4)
    second = lax.rem(2 * sequence + 5 - place[0], 4)
    out_ref[first, rows, 0:rank] = dot(v_ref[0], wv_ref[...], NT)
    out_ref[first, rows, rank:LANES] = dot(a_ref[0], wa_ref[...], NT)
    out_ref[second, rows, 0:rank] = dot(g_ref[0], wg_ref[...], NT)
    out_ref[second, rows, rank:LANES] = dot(m_ref[0], wm_ref[...], NT)


def project(place, acts, weights, tokens):
    sequences, length, _ = acts[0].shape
    half = length // 2
    blocks = half // tokens
    act_specs = [pl.BlockSpec((1, tokens, a.shape[2]), lambda e, b, s: (e, s[1] * blocks + b, 0)) for a in acts]
    weight_specs = [pl.BlockSpec(w.shape, lambda e, b, s: (0, 0)) for w in weights]
    flops = 2 * sequences * half * sum(w.size for w in weights)
    return pl.pallas_call(
        project_kernel,
        grid_spec=pltpu.PrefetchScalarGridSpec(
            num_scalar_prefetch=1,
            grid=(sequences, blocks),
            in_specs=act_specs + weight_specs,
            out_specs=pl.BlockSpec((4, half, LANES), lambda e, b, s: (0, 0, 0)),
        ),
        out_shape=jax.ShapeDtypeStruct((4, half, LANES), F32),
        cost_estimate=pl.CostEstimate(flops=flops, bytes_accessed=sum(a.size for a in acts) + 4 * half * LANES * 4, transcendentals=0),
        compiler_params=pltpu.CompilerParams(vmem_limit_bytes=58 * 2**20),
        name="project",
    )(place, *acts, *weights)


def add_kernel(own_ref, other_ref, *out_refs):
    for slot, out_ref in enumerate(out_refs):
        out_ref[...] = own_ref[slot] + other_ref[slot]


def add_cores(own, other):
    shape = jax.ShapeDtypeStruct(own.shape[1:], F32)
    return pl.pallas_call(
        add_kernel,
        out_shape=[shape] * 4,
        in_specs=[pl.BlockSpec(memory_space=VMEM)] * 2,
        out_specs=[pl.BlockSpec(memory_space=VMEM)] * 4,
        cost_estimate=pl.CostEstimate(flops=own.size, bytes_accessed=12 * own.size, transcendentals=0),
        compiler_params=pltpu.CompilerParams(vmem_limit_bytes=8 * 2**20),
        name="add_cores",
    )(own, other)


def outer_kernel(rank, a_ref, b_ref, c_ref, d_ref, out_ref, held):
    vectors = ((a_ref[...] + b_ref[...]) + (c_ref[...] + d_ref[...])).astype(BF16)
    held[...] = dot(vectors[:, 0:rank], vectors, TN)
    even = held[pl.ds(0, rank // 2, stride=2), :]
    odd = held[pl.ds(1, rank // 2, stride=2), :]
    lane = lax.broadcasted_iota(jnp.int32, even.shape, 1)
    rows = jnp.where(lane < rank, pltpu.roll(even, rank, 1), odd)
    for target in range(out_ref.shape[0]):
        out_ref[target] = rows


def outer(parts, rank, width):
    return pl.pallas_call(
        functools.partial(outer_kernel, rank),
        out_shape=jax.ShapeDtypeStruct((width, rank // 2, LANES), F32),
        in_specs=[pl.BlockSpec(memory_space=VMEM)] * 4,
        out_specs=pl.BlockSpec(memory_space=VMEM),
        scratch_shapes=[pltpu.VMEM((rank, LANES), F32)],
        compiler_params=pltpu.CompilerParams(vmem_limit_bytes=8 * 2**20),
        name="outer",
    )(*parts)


def features_kernel(scale, place, sums_ref, send_ref, norm_ref):
    blocks = send_ref.shape[0]
    feats = {}
    squares = {}
    for e in range(2):
        for p in range(2):
            chip = 2 * e + p
            rounded = ((sums_ref[2 * chip] + sums_ref[2 * chip + 1]) * scale).astype(BF16)
            wide = rounded.astype(F32)
            feats[e, p] = wide
            squares[e, p] = jnp.sum(jnp.sum(wide * wide, axis=1, keepdims=True), axis=0, keepdims=True)
    for e in range(2):
        mean = (squares[e, 0] + squares[e, 1]) / (2.0 * blocks * LANES)
        norm_ref[e : e + 1, :] = jnp.broadcast_to(jnp.sqrt(mean + 1e-06), (1, LANES))
    row = lax.broadcasted_iota(jnp.int32, (16, LANES), 0)
    for p in range(2):
        total = squares[0, p] + squares[1, p]
        high = total.astype(BF16).astype(F32)
        middle = (total - high).astype(BF16).astype(F32)
        low = total - high - middle
        base = jnp.zeros((16, LANES), F32)
        for e in range(2):
            for k in range(4):
                at = place[1] * 4 + k
                base = jnp.where(row == 5 * e + 1 + k, rounded_row(sums_ref, scale, 2 * e + p, at), base)
        for k, term in enumerate((high, middle, low)):
            base = jnp.where(row == 10 + k, term, base)
        for i in range(blocks):
            tile = jnp.where(row == 0, feats[0, p][i : i + 1, :], base)
            tile = jnp.where(row == 5, feats[1, p][i : i + 1, :], tile)
            send_ref[i, p] = tile.astype(BF16)


def rounded_row(sums_ref, scale, chip, at):
    summed = sums_ref[2 * chip, pl.ds(at, 1), :] + sums_ref[2 * chip + 1, pl.ds(at, 1), :]
    return (summed * scale).astype(BF16).astype(F32)


def features(place, sums, scale, dp):
    blocks = sums.shape[1]
    return pl.pallas_call(
        functools.partial(features_kernel, scale),
        out_shape=[
            jax.ShapeDtypeStruct((dp, 2, 16, LANES), BF16),
            jax.ShapeDtypeStruct((2, LANES), F32),
        ],
        in_specs=[pl.BlockSpec(memory_space=pltpu.SMEM), pl.BlockSpec(memory_space=VMEM)],
        out_specs=[pl.BlockSpec(memory_space=VMEM)] * 2,
        compiler_params=pltpu.CompilerParams(vmem_limit_bytes=8 * 2**20),
        name="features",
    )(place, sums)


def fisher_kernel(examples, place, got_ref, out_ref, held):
    sources = got_ref.shape[0]
    count = examples * 32 * LANES
    row = lax.broadcasted_iota(jnp.int32, (LANES, LANES), 0)
    lane = lax.broadcasted_iota(jnp.int32, (LANES, LANES), 1)
    for p in range(2):
        held[...] = got_ref[:, p].astype(F32).reshape(sources * 16, LANES)

        def pick(r):
            return held[pl.ds(r, sources, stride=16), :]

        mine = jnp.concatenate([pick(0), pick(5)], axis=0).astype(BF16)
        total = jnp.sum(pick(10) + pick(11) + pick(12), axis=0, keepdims=True)
        damping = 0.5 * total / count
        for k in range(4):
            theirs = jnp.concatenate([pick(1 + k), pick(6 + k)], axis=0).astype(BF16)
            block = dot(mine, theirs, TN) * (1.0 / examples)
            on = jnp.logical_and(row == lane, place[0] - 4 * place[1] == k)
            out_ref[:, p, k * LANES : (k + 1) * LANES] = block + jnp.where(on, damping, 0.0)


def fisher_block(place, got, examples):
    return pl.pallas_call(
        functools.partial(fisher_kernel, examples),
        out_shape=jax.ShapeDtypeStruct((LANES, 2, 4 * LANES), F32),
        in_specs=[pl.BlockSpec(memory_space=pltpu.SMEM), pl.BlockSpec(memory_space=VMEM)],
        out_specs=pl.BlockSpec(memory_space=VMEM),
        scratch_shapes=[pltpu.VMEM((got.shape[0] * 16, LANES), F32)],
        compiler_params=pltpu.CompilerParams(vmem_limit_bytes=8 * 2**20),
        name="fisher",
    )(place, got)


def scores_kernel(got_ref, query_ref, out_ref, held):
    sources = got_ref.shape[0]
    total = None
    for p in range(2):
        held[...] = got_ref[:, p].astype(F32).reshape(sources * 16, LANES)
        pair = [held[pl.ds(5 * e, sources, stride=16), :] for e in range(2)]
        part = dot(jnp.concatenate(pair, axis=0).astype(BF16), query_ref[p], NT)
        total = part if total is None else total + part
    out_ref[:, 0, :] = total[0:sources]
    out_ref[:, 1, :] = total[sources:]


def score_shares(got, query):
    sources = got.shape[0]
    return pl.pallas_call(
        scores_kernel,
        out_shape=jax.ShapeDtypeStruct((sources, 2, query.shape[1]), F32),
        in_specs=[pl.BlockSpec(memory_space=VMEM)] * 2,
        out_specs=pl.BlockSpec(memory_space=VMEM),
        scratch_shapes=[pltpu.VMEM((sources * 16, LANES), F32)],
        compiler_params=pltpu.CompilerParams(vmem_limit_bytes=8 * 2**20),
        name="score_shares",
    )(got, query)


def shards(
    attn_in,
    v_grad,
    mlp_hidden,
    out_grad,
    proj_in_attn,
    proj_out_value,
    proj_in_mlp,
    proj_out_mlp,
    query_features,
):
    rank = proj_in_attn.shape[0]
    length = attn_in.shape[1]
    dp = lax.axis_size("dp")
    width = lax.axis_size("tensor")
    examples = attn_in.shape[0] * dp
    dp_pos = lax.axis_index("dp")
    tp_pos = lax.axis_index("tensor")
    chip, core = tp_pos // 2, tp_pos % 2

    acts = (v_grad, attn_in, out_grad, mlp_hidden)
    weights = (proj_out_value, proj_in_attn, proj_out_mlp, proj_in_mlp)
    theirs = project(jnp.stack([chip, 1 - core]).astype(jnp.int32), acts, weights, 256)
    other = lax.ppermute(theirs, "tensor", [(k, k ^ 1) for k in range(width)])
    own = project(jnp.stack([chip, core]).astype(jnp.int32), acts, weights, 256)
    kept, *sent = add_cores(own, other)
    parts = [kept] + [
        lax.ppermute(sent[s - 1], "tensor", [(k, (k + 2 * s) % width) for k in range(width)]) for s in (1, 2, 3)
    ]
    partial = outer(parts, rank, width)
    sums = lax.all_to_all(partial, "tensor", 0, 0, tiled=True)
    place = jnp.stack([dp_pos, tp_pos]).astype(jnp.int32)
    send, norms = features(place, sums, 1.0 / math.sqrt(length), dp)
    got = lax.all_to_all(send, "dp", 0, 0, tiled=True)
    shares = lax.all_to_all(score_shares(got, query_features), "dp", 0, 0, tiled=True)
    fisher = fisher_block(place, got, examples)
    scores = jnp.sum(shares, axis=0) / norms[:, 0:1]
    return (fisher, scores)


def solution(mesh):
    return jax.shard_map(
        shards,
        mesh=mesh,
        in_specs=(
            P("dp", None, "tensor"),
            P("dp", None, "tensor"),
            P("dp", None, "tensor"),
            P("dp", None, "tensor"),
            P(None, "tensor"),
            P(None, "tensor"),
            P(None, "tensor"),
            P(None, "tensor"),
            P(None, "tensor", "dp"),
        ),
        out_specs=(P("dp", None, "tensor"), P("dp", "tensor")),
        check_vma=False,
    )
```

```python
import functools
import math

import jax
import jax.numpy as jnp
from jax import lax
from jax.experimental import pallas as pl
from jax.experimental.pallas import tpu as pltpu
from jax.sharding import PartitionSpec as P

F32 = jnp.float32
BF16 = jnp.bfloat16
LANES = 128
VMEM = pltpu.VMEM
NT = (((1,), (1,)), ((), ()))
TN = (((0,), (0,)), ((), ()))


def dot(a, b, dims):
    return lax.dot_general(a, b, dims, preferred_element_type=F32)


def project_kernel(place, v, a, g, m, wv, wa, wg, wm, theirs_ref, own_ref, sv, sa, sg, sm, swv, swa, swg, swm, held, sems, weight_sems):
    arrays, buffers = (v, a, g, m), (sv, sa, sg, sm)
    weights, weight_buffers = (wv, wa, wg, wm), (swv, swa, swg, swm)
    half = v.shape[1] // 2
    rank = wv.shape[0]
    chip, core = place[0], place[1]

    def weight_copy(i):
        return pltpu.make_async_copy(weights[i], weight_buffers[i], weight_sems.at[i])

    def copy(i, chunk):
        which = lax.rem(core + 1 + chunk // 2, 2)
        start = pl.multiple_of(which * half, half)
        return pltpu.make_async_copy(arrays[i].at[chunk % 2, pl.ds(start, half)], buffers[i].at[chunk], sems.at[chunk, i])

    for i in range(4):
        weight_copy(i).start()
    for chunk in range(2):
        for i in range(4):
            copy(i, chunk).start()
    for i in range(4):
        weight_copy(i).wait()

    def work(chunk, carry):
        for i in range(4):
            copy(i, chunk).wait()

        @pl.when(chunk < 2)
        def _():
            for i in range(4):
                copy(i, chunk + 2).start()

        for i in range(4):
            slot = lax.rem(2 * lax.rem(chunk, 2) + i // 2 + 4 - chip, 4)
            held[chunk // 2, slot, :, (i % 2) * rank : (i % 2 + 1) * rank] = dot(buffers[i][chunk], weight_buffers[i][...], NT)
        return carry

    lax.fori_loop(0, 4, work, 0)
    theirs_ref[...] = held[0]
    own_ref[...] = held[1]


def project(place, acts, weights):
    sequences, length, _ = acts[0].shape
    half = length // 2
    hbm = pl.BlockSpec(memory_space=pltpu.HBM)
    flops = 2 * sequences * length * sum(w.size for w in weights)
    held_apart = [pltpu.with_memory_space_constraint(x, pltpu.HBM) for x in (*acts, *weights)]
    return pl.pallas_call(
        project_kernel,
        out_shape=[pltpu.VMEM((4, half, LANES), F32)] * 2,
        in_specs=[pl.BlockSpec(memory_space=pltpu.SMEM)] + [hbm] * 8,
        out_specs=[pl.BlockSpec(memory_space=VMEM)] * 2,
        scratch_shapes=[pltpu.VMEM((4, half, a.shape[2]), BF16) for a in acts]
        + [pltpu.VMEM(w.shape, BF16) for w in weights]
        + [pltpu.VMEM((2, 4, half, LANES), F32), pltpu.SemaphoreType.DMA((4, 4)), pltpu.SemaphoreType.DMA((4,))],
        cost_estimate=pl.CostEstimate(flops=flops, bytes_accessed=2 * sum(a.size for a in acts), transcendentals=0),
        compiler_params=pltpu.CompilerParams(vmem_limit_bytes=32 * 2**20),
        name="project",
    )(place, *held_apart)


def add_kernel(own_ref, other_ref, *out_refs):
    for slot, out_ref in enumerate(out_refs):
        out_ref[...] = own_ref[slot] + other_ref[slot]


def add_cores(own, other):
    return pl.pallas_call(
        add_kernel,
        out_shape=[jax.ShapeDtypeStruct(own.shape[1:], F32)] * 4,
        in_specs=[pl.BlockSpec(memory_space=VMEM)] * 2,
        out_specs=[pl.BlockSpec(memory_space=VMEM)] * 4,
        cost_estimate=pl.CostEstimate(flops=own.size, bytes_accessed=12 * own.size, transcendentals=0),
        compiler_params=pltpu.CompilerParams(vmem_limit_bytes=8 * 2**20),
        name="add_cores",
    )(own, other)


def outer_kernel(rank, a_ref, b_ref, c_ref, d_ref, out_ref, held):
    vectors = ((a_ref[...] + b_ref[...]) + (c_ref[...] + d_ref[...])).astype(BF16)
    held[...] = dot(vectors[:, 0:rank], vectors, TN)
    even = held[pl.ds(0, rank // 2, stride=2), :]
    odd = held[pl.ds(1, rank // 2, stride=2), :]
    lane = lax.broadcasted_iota(jnp.int32, even.shape, 1)
    rows = jnp.where(lane < rank, pltpu.roll(even, rank, 1), odd)
    for target in range(out_ref.shape[0]):
        out_ref[target] = rows


def outer(parts, rank, width):
    return pl.pallas_call(
        functools.partial(outer_kernel, rank),
        out_shape=jax.ShapeDtypeStruct((width, rank // 2, LANES), F32),
        in_specs=[pl.BlockSpec(memory_space=VMEM)] * 4,
        out_specs=pl.BlockSpec(memory_space=VMEM),
        scratch_shapes=[pltpu.VMEM((rank, LANES), F32)],
        compiler_params=pltpu.CompilerParams(vmem_limit_bytes=8 * 2**20),
        name="outer",
    )(*parts)


def features_kernel(scale, place, sums_ref, send_ref, norm_ref, *share_refs):
    *share_refs, feat_ref = share_refs
    blocks = send_ref.shape[0]
    feats = {}
    squares = {}
    for e in range(2):
        for p in range(2):
            chip = 2 * e + p
            rounded = ((sums_ref[2 * chip] + sums_ref[2 * chip + 1]) * scale).astype(BF16)
            wide = rounded.astype(F32)
            feats[e, p] = wide
            feat_ref[e, p] = wide
            squares[e, p] = jnp.sum(jnp.sum(wide * wide, axis=1, keepdims=True), axis=0, keepdims=True)
    for e in range(2):
        mean = (squares[e, 0] + squares[e, 1]) / (2.0 * blocks * LANES)
        norm_ref[e : e + 1, :] = jnp.broadcast_to(jnp.sqrt(mean + 1e-06), (1, LANES))
    planes = len(share_refs)
    depth = blocks // planes
    for turn, share_ref in enumerate(share_refs):
        start = pl.multiple_of(lax.rem(place[0] // depth + turn, planes) * depth, depth)
        for e in range(2):
            for p in range(2):
                share_ref[e, p * depth : (p + 1) * depth, :] = feat_ref[e, p, pl.ds(start, depth), :]
    row = lax.broadcasted_iota(jnp.int32, (16, LANES), 0)
    for p in range(2):
        total = squares[0, p] + squares[1, p]
        high = total.astype(BF16).astype(F32)
        middle = (total - high).astype(BF16).astype(F32)
        low = total - high - middle
        base = jnp.zeros((16, LANES), F32)
        for e in range(2):
            for k in range(4):
                at = place[1] * 4 + k
                base = jnp.where(row == 5 * e + 1 + k, rounded_row(sums_ref, scale, 2 * e + p, at), base)
        for k, term in enumerate((high, middle, low)):
            base = jnp.where(row == 10 + k, term, base)
        for i in range(blocks):
            tile = jnp.where(row == 0, feats[0, p][i : i + 1, :], base)
            tile = jnp.where(row == 5, feats[1, p][i : i + 1, :], tile)
            send_ref[i, p] = tile.astype(BF16)


def rounded_row(sums_ref, scale, chip, at):
    summed = sums_ref[2 * chip, pl.ds(at, 1), :] + sums_ref[2 * chip + 1, pl.ds(at, 1), :]
    return (summed * scale).astype(BF16).astype(F32)


def features(place, sums, scale, dp, planes):
    blocks = sums.shape[1]
    return pl.pallas_call(
        functools.partial(features_kernel, scale),
        out_shape=[
            jax.ShapeDtypeStruct((dp, 2, 16, LANES), BF16),
            jax.ShapeDtypeStruct((2, LANES), F32),
        ]
        + [jax.ShapeDtypeStruct((2, 2 * blocks // planes, LANES), F32)] * planes,
        in_specs=[pl.BlockSpec(memory_space=pltpu.SMEM), pl.BlockSpec(memory_space=VMEM)],
        out_specs=[pl.BlockSpec(memory_space=VMEM)] * (2 + planes),
        scratch_shapes=[pltpu.VMEM((2, 2, blocks, LANES), F32)],
        compiler_params=pltpu.CompilerParams(vmem_limit_bytes=8 * 2**20),
        name="features",
    )(place, sums)


def fisher_kernel(examples, place, got_ref, out_ref, held):
    sources = got_ref.shape[0]
    count = examples * 32 * LANES
    row = lax.broadcasted_iota(jnp.int32, (LANES, LANES), 0)
    lane = lax.broadcasted_iota(jnp.int32, (LANES, LANES), 1)
    for p in range(2):
        held[...] = got_ref[:, p].astype(F32).reshape(sources * 16, LANES)

        def pick(r):
            return held[pl.ds(r, sources, stride=16), :]

        mine = jnp.concatenate([pick(0), pick(5)], axis=0).astype(BF16)
        total = jnp.sum(pick(10) + pick(11) + pick(12), axis=0, keepdims=True)
        damping = 0.5 * total / count
        for k in range(4):
            theirs = jnp.concatenate([pick(1 + k), pick(6 + k)], axis=0).astype(BF16)
            block = dot(mine, theirs, TN) * (1.0 / examples)
            on = jnp.logical_and(row == lane, place[0] - 4 * place[1] == k)
            out_ref[:, p, k * LANES : (k + 1) * LANES] = block + jnp.where(on, damping, 0.0)


def fisher_block(place, got, examples):
    return pl.pallas_call(
        functools.partial(fisher_kernel, examples),
        out_shape=jax.ShapeDtypeStruct((LANES, 2, 4 * LANES), F32),
        in_specs=[pl.BlockSpec(memory_space=pltpu.SMEM), pl.BlockSpec(memory_space=VMEM)],
        out_specs=pl.BlockSpec(memory_space=VMEM),
        scratch_shapes=[pltpu.VMEM((got.shape[0] * 16, LANES), F32)],
        compiler_params=pltpu.CompilerParams(vmem_limit_bytes=8 * 2**20),
        name="fisher",
    )(place, got)


def scores_kernel(distances, place, *refs):
    queries = len(distances)
    query_refs, refs = refs[:queries], refs[queries:]
    planes = (len(refs) - 1) // 2
    share_refs, out_refs, held = refs[:planes], refs[planes:-1], refs[-1]
    depth = sum(len(d) for d in distances)
    z = lax.rem(place[0], depth)
    rows = 2 * depth
    for turn, share_ref in enumerate(share_refs):
        for e in range(2):
            held[(2 * turn + e) * rows : (2 * turn + e + 1) * rows, :] = share_ref[e]
    total = None
    for query_ref, group in zip(query_refs, distances):
        for at, distance in enumerate(group):
            source = lax.rem(z + depth - distance, depth)
            for p in range(2):
                vectors = held[pl.ds(p * depth + source, 2 * planes, stride=rows), :].astype(BF16)
                part = dot(vectors, query_ref[at, p], NT)
                total = part if total is None else total + part
    for turn, out_ref in enumerate(out_refs):
        out_ref[...] = total[2 * turn : 2 * turn + 2, :]


def score_shares(place, queries, distances, shares):
    planes = len(shares)
    vmem = pl.BlockSpec(memory_space=VMEM)
    size = sum(q.size for q in queries)
    return pl.pallas_call(
        functools.partial(scores_kernel, distances),
        out_shape=[jax.ShapeDtypeStruct((2, queries[0].shape[2]), F32)] * planes,
        in_specs=[pl.BlockSpec(memory_space=pltpu.SMEM)] + [vmem] * (len(queries) + planes),
        out_specs=[vmem] * planes,
        scratch_shapes=[pltpu.VMEM((2 * planes * shares[0].shape[1], LANES), F32)],
        cost_estimate=pl.CostEstimate(flops=16 * size, bytes_accessed=2 * size, transcendentals=0),
        compiler_params=pltpu.CompilerParams(vmem_limit_bytes=8 * 2**20),
        name="score_shares",
    )(place, *queries, *shares)


def shards(
    attn_in,
    v_grad,
    mlp_hidden,
    out_grad,
    proj_in_attn,
    proj_out_value,
    proj_in_mlp,
    proj_out_mlp,
    query_features,
):
    rank = proj_in_attn.shape[0]
    length = attn_in.shape[1]
    dp = lax.axis_size("dp")
    width = lax.axis_size("tensor")
    examples = attn_in.shape[0] * dp
    dp_pos = lax.axis_index("dp")
    tp_pos = lax.axis_index("tensor")
    chip, core = tp_pos // 2, tp_pos % 2

    planes, depth = 4, dp // 4

    def along_z(x, turn):
        return lax.ppermute(x, "dp", [(k, k // depth * depth + (k + turn) % depth) for k in range(dp)])

    def along_y(x, turn):
        return lax.ppermute(x, "dp", [(k, (k + turn * depth) % dp) for k in range(dp)])

    distances, queries = [[0]], [query_features[None]]

    def widen():
        reach = depth // 2 ** len(queries)
        queries.append(along_z(jnp.concatenate(queries, axis=0) if len(queries) > 1 else queries[0], reach))
        distances.append([d + reach for group in distances for d in group])

    widen()
    acts = (v_grad, attn_in, out_grad, mlp_hidden)
    weights = (proj_out_value, proj_in_attn, proj_out_mlp, proj_in_mlp)
    theirs, own = project(jnp.stack([chip, core]).astype(jnp.int32), acts, weights)
    theirs, own, queries[1] = lax.optimization_barrier((theirs, own, queries[1]))
    other = lax.ppermute(theirs, "tensor", [(k, k ^ 1) for k in range(width)])
    kept, *sent = add_cores(own, other)
    widen()
    parts = [kept] + [
        lax.ppermute(sent[s - 1], "tensor", [(k, (k + 2 * s) % width) for k in range(width)]) for s in (1, 2, 3)
    ]
    parts[2], queries[2] = lax.optimization_barrier((parts[2], queries[2]))
    widen()
    partial = outer(parts, rank, width)
    sums = lax.all_to_all(partial, "tensor", 0, 0, tiled=True)
    sums, queries[3] = lax.optimization_barrier((sums, queries[3]))
    place = jnp.stack([dp_pos, tp_pos]).astype(jnp.int32)
    send, norms, *shares = features(place, sums, 1.0 / math.sqrt(length), dp, planes)
    shares = [shares[0]] + [along_y(shares[turn], turn) for turn in range(1, planes)]
    got = lax.all_to_all(send, "dp", 0, 0, tiled=True)
    scored = list(score_shares(place, queries, distances, shares))
    scored[0], got = lax.optimization_barrier((scored[0], got))
    fisher = fisher_block(place, got, examples)
    scored = [scored[0]] + [along_y(scored[turn], -turn) for turn in range(1, planes)]
    scores = sum(scored) / norms
    return (fisher, scores)


def solution(mesh):
    return jax.shard_map(
        shards,
        mesh=mesh,
        in_specs=(
            P("dp", None, "tensor"),
            P("dp", None, "tensor"),
            P("dp", None, "tensor"),
            P("dp", None, "tensor"),
            P(None, "tensor"),
            P(None, "tensor"),
            P(None, "tensor"),
            P(None, "tensor"),
            P(None, "tensor", "dp"),
        ),
        out_specs=(P("dp", None, "tensor"), P("dp", "tensor")),
        check_vma=False,
    )
```

```python
import functools
import math

import jax
import jax.numpy as jnp
from jax import lax
from jax.experimental import pallas as pl
from jax.experimental.pallas import tpu as pltpu
from jax.sharding import PartitionSpec as P

F32 = jnp.float32
BF16 = jnp.bfloat16
LANES = 128
VMEM = pltpu.VMEM
NT = (((1,), (1,)), ((), ()))
TN = (((0,), (0,)), ((), ()))


def dot(a, b, dims):
    return lax.dot_general(a, b, dims, preferred_element_type=F32)


def project_kernel(place, v, a, g, m, wv, wa, wg, wm, theirs_ref, own_ref, value, down, value_weights, down_weights, sems, weight_sems):
    arrays, buffers = (v, a, g, m), (value, value, down, down)
    weights, weight_buffers = (wv, wa, wg, wm), (value_weights, value_weights, down_weights, down_weights)
    half = v.shape[1] // 2
    rank = wv.shape[0]
    chip, core = place[0], place[1]

    def columns(i):
        return pl.ds(0, arrays[i].shape[2]) if i % 2 == 0 else pl.ds(arrays[i - 1].shape[2], arrays[i].shape[2])

    def weight_copy(i):
        target = weight_buffers[i].at[pl.ds(i % 2 * rank, rank), columns(i)]
        return pltpu.make_async_copy(weights[i], target, weight_sems.at[i])

    def copy(i, chunk):
        which = lax.rem(core + 1 + chunk // 2, 2)
        start = pl.multiple_of(which * half, half)
        target = buffers[i].at[chunk, :, columns(i)]
        return pltpu.make_async_copy(arrays[i].at[chunk % 2, pl.ds(start, half)], target, sems.at[chunk, i])

    for i in range(4):
        weight_copy(i).start()
    for chunk in range(2):
        for i in range(4):
            copy(i, chunk).start()
    for i in range(4):
        weight_buffers[i][pl.ds((1 - i % 2) * rank, rank), columns(i)] = jnp.zeros((rank, arrays[i].shape[2]), BF16)
    for i in range(4):
        weight_copy(i).wait()

    def work(out_ref, chunk, carry):
        for i in range(4):
            copy(i, chunk).wait()

        @pl.when(chunk < 2)
        def _():
            for i in range(4):
                copy(i, chunk + 2).start()

        for p, (inputs, matrix) in enumerate(((value, value_weights), (down, down_weights))):
            slot = lax.rem(2 * lax.rem(chunk, 2) + p + 4 - chip, 4)
            out_ref[slot] = dot(inputs[chunk], matrix[...], NT)
        return carry

    lax.fori_loop(0, 2, functools.partial(work, theirs_ref), 0)
    lax.fori_loop(2, 4, functools.partial(work, own_ref), 0)


def project(place, acts, weights):
    sequences, length, _ = acts[0].shape
    half = length // 2
    rank = weights[0].shape[0]
    hbm = pl.BlockSpec(memory_space=pltpu.HBM)
    flops = 2 * sequences * length * sum(w.size for w in weights)
    held_apart = [pltpu.with_memory_space_constraint(x, pltpu.HBM) for x in (*acts, *weights)]
    widths = [acts[0].shape[2] + acts[1].shape[2], acts[2].shape[2] + acts[3].shape[2]]
    return pl.pallas_call(
        project_kernel,
        out_shape=[pltpu.VMEM((4, half, LANES), F32)] * 2,
        in_specs=[pl.BlockSpec(memory_space=pltpu.SMEM)] + [hbm] * 8,
        out_specs=[pl.BlockSpec(memory_space=VMEM)] * 2,
        scratch_shapes=[pltpu.VMEM((4, half, width), BF16) for width in widths]
        + [pltpu.VMEM((2 * rank, width), BF16) for width in widths]
        + [pltpu.SemaphoreType.DMA((4, 4)), pltpu.SemaphoreType.DMA((4,))],
        cost_estimate=pl.CostEstimate(flops=flops, bytes_accessed=2 * sum(a.size for a in acts), transcendentals=0),
        compiler_params=pltpu.CompilerParams(vmem_limit_bytes=32 * 2**20),
        name="project",
    )(place, *held_apart)


def add_kernel(own_ref, other_ref, *out_refs):
    for slot, out_ref in enumerate(out_refs):
        out_ref[...] = own_ref[slot] + other_ref[slot]


def add_cores(own, other):
    return pl.pallas_call(
        add_kernel,
        out_shape=[jax.ShapeDtypeStruct(own.shape[1:], F32)] * 4,
        in_specs=[pl.BlockSpec(memory_space=VMEM)] * 2,
        out_specs=[pl.BlockSpec(memory_space=VMEM)] * 4,
        cost_estimate=pl.CostEstimate(flops=own.size, bytes_accessed=12 * own.size, transcendentals=0),
        compiler_params=pltpu.CompilerParams(vmem_limit_bytes=8 * 2**20),
        name="add_cores",
    )(own, other)


def outer_kernel(rank, a_ref, b_ref, c_ref, d_ref, out_ref, held):
    vectors = ((a_ref[...] + b_ref[...]) + (c_ref[...] + d_ref[...])).astype(BF16)
    held[...] = dot(vectors[:, 0:rank], vectors, TN)
    even = held[pl.ds(0, rank // 2, stride=2), :]
    odd = held[pl.ds(1, rank // 2, stride=2), :]
    lane = lax.broadcasted_iota(jnp.int32, even.shape, 1)
    rows = jnp.where(lane < rank, pltpu.roll(even, rank, 1), odd)
    for target in range(out_ref.shape[0]):
        out_ref[target] = rows


def outer(parts, rank, width):
    return pl.pallas_call(
        functools.partial(outer_kernel, rank),
        out_shape=pltpu.VMEM((width, rank // 2, LANES), F32),
        in_specs=[pl.BlockSpec(memory_space=VMEM)] * 4,
        out_specs=pl.BlockSpec(memory_space=VMEM),
        scratch_shapes=[pltpu.VMEM((rank, LANES), F32)],
        compiler_params=pltpu.CompilerParams(vmem_limit_bytes=8 * 2**20),
        name="outer",
    )(*parts)


def features_kernel(scale, place, sums_ref, send_ref, norm_ref, *share_refs):
    *share_refs, feat_ref = share_refs
    blocks = send_ref.shape[0]
    feats = {}
    squares = {}
    for e in range(2):
        for p in range(2):
            chip = 2 * e + p
            rounded = ((sums_ref[2 * chip] + sums_ref[2 * chip + 1]) * scale).astype(BF16)
            wide = rounded.astype(F32)
            feats[e, p] = wide
            feat_ref[e, p] = wide
            squares[e, p] = jnp.sum(jnp.sum(wide * wide, axis=1, keepdims=True), axis=0, keepdims=True)
    for e in range(2):
        mean = (squares[e, 0] + squares[e, 1]) / (2.0 * blocks * LANES)
        norm_ref[e : e + 1, :] = jnp.broadcast_to(jnp.sqrt(mean + 1e-06), (1, LANES))
    planes = len(share_refs)
    depth = blocks // planes
    for turn, share_ref in enumerate(share_refs):
        start = pl.multiple_of(lax.rem(place[2] // depth + turn, planes) * depth, depth)
        for e in range(2):
            for p in range(2):
                share_ref[e, p * depth : (p + 1) * depth, :] = feat_ref[e, p, pl.ds(start, depth), :]
    row = lax.broadcasted_iota(jnp.int32, (16, LANES), 0)
    for p in range(2):
        total = squares[0, p] + squares[1, p]
        high = total.astype(BF16).astype(F32)
        middle = (total - high).astype(BF16).astype(F32)
        low = total - high - middle
        base = jnp.zeros((16, LANES), F32)
        for e in range(2):
            for k in range(4):
                at = place[3] * 4 + k
                base = jnp.where(row == 5 * e + 1 + k, rounded_row(sums_ref, scale, 2 * e + p, at), base)
        for k, term in enumerate((high, middle, low)):
            base = jnp.where(row == 10 + k, term, base)
        for i in range(blocks):
            tile = jnp.where(row == 0, feats[0, p][i : i + 1, :], base)
            tile = jnp.where(row == 5, feats[1, p][i : i + 1, :], tile)
            send_ref[i, p] = tile.astype(BF16)


def rounded_row(sums_ref, scale, chip, at):
    summed = sums_ref[2 * chip, pl.ds(at, 1), :] + sums_ref[2 * chip + 1, pl.ds(at, 1), :]
    return (summed * scale).astype(BF16).astype(F32)


def features(place, sums, scale, dp, planes):
    blocks = sums.shape[1]
    return pl.pallas_call(
        functools.partial(features_kernel, scale),
        out_shape=[
            pltpu.VMEM((dp, 2, 16, LANES), BF16),
            pltpu.VMEM((2, LANES), F32),
        ]
        + [pltpu.VMEM((2, 2 * blocks // planes, LANES), F32)] * planes,
        in_specs=[pl.BlockSpec(memory_space=pltpu.SMEM), pl.BlockSpec(memory_space=VMEM)],
        out_specs=[pl.BlockSpec(memory_space=VMEM)] * (2 + planes),
        scratch_shapes=[pltpu.VMEM((2, 2, blocks, LANES), F32)],
        compiler_params=pltpu.CompilerParams(vmem_limit_bytes=8 * 2**20),
        name="features",
    )(place, sums)


def fisher_kernel(examples, place, got_ref, out_ref, held):
    sources = got_ref.shape[0]
    count = examples * 32 * LANES
    row = lax.broadcasted_iota(jnp.int32, (LANES, LANES), 0)
    lane = lax.broadcasted_iota(jnp.int32, (LANES, LANES), 1)
    for p in range(2):
        held[...] = got_ref[:, p].astype(F32).reshape(sources * 16, LANES)

        def pick(r):
            return held[pl.ds(r, sources, stride=16), :]

        mine = jnp.concatenate([pick(0), pick(5)], axis=0).astype(BF16)
        theirs = [jnp.concatenate([pick(1 + k), pick(6 + k)], axis=0) for k in range(4)]
        total = jnp.sum(pick(10) + pick(11) + pick(12), axis=0, keepdims=True)
        damping = 0.5 * total / count
        blocks = dot(mine, jnp.concatenate(theirs, axis=1).astype(BF16), TN) * (1.0 / examples)
        for k in range(4):
            on = jnp.logical_and(row == lane, place[2] - 4 * place[3] == k)
            made = blocks[:, k * LANES : (k + 1) * LANES] + jnp.where(on, damping, 0.0)
            out_ref[pl.ds(2 * k + p, LANES, stride=8), :] = made


def fisher_block(place, got, examples):
    made = pl.pallas_call(
        functools.partial(fisher_kernel, examples),
        out_shape=jax.ShapeDtypeStruct((8 * LANES, LANES), F32),
        in_specs=[pl.BlockSpec(memory_space=pltpu.SMEM), pl.BlockSpec(memory_space=VMEM)],
        out_specs=pl.BlockSpec(memory_space=VMEM),
        scratch_shapes=[pltpu.VMEM((got.shape[0] * 16, LANES), F32)],
        compiler_params=pltpu.CompilerParams(vmem_limit_bytes=8 * 2**20),
        name="fisher",
    )(place, got)
    return made.reshape(LANES, 4, 2, LANES).transpose(0, 2, 1, 3).reshape(LANES, 2, 4 * LANES)


def scores_kernel(distances, place, *refs):
    queries = len(distances)
    query_refs, refs = refs[:queries], refs[queries:]
    planes = (len(refs) - 1) // 2
    share_refs, out_refs, held = refs[:planes], refs[planes:-1], refs[-1]
    depth = sum(len(d) for d in distances)
    z = lax.rem(place[2], depth)
    rows = 2 * depth
    for turn, share_ref in enumerate(share_refs):
        for e in range(2):
            held[(2 * turn + e) * rows : (2 * turn + e + 1) * rows, :] = share_ref[e]
    total = None
    for query_ref, group in zip(query_refs, distances):
        for at, distance in enumerate(group):
            source = lax.rem(z + depth - distance, depth)
            vectors = [held[pl.ds(p * depth + source, 2 * planes, stride=rows), :] for p in range(2)]
            wanted = [query_ref[at, p] for p in range(2)]
            part = dot(jnp.concatenate(vectors, axis=1).astype(BF16), jnp.concatenate(wanted, axis=1), NT)
            total = part if total is None else total + part
    for turn, out_ref in enumerate(out_refs):
        out_ref[...] = total[2 * turn : 2 * turn + 2, :]


def score_shares(place, queries, distances, shares):
    planes = len(shares)
    vmem = pl.BlockSpec(memory_space=VMEM)
    size = sum(q.size for q in queries)
    return pl.pallas_call(
        functools.partial(scores_kernel, distances),
        out_shape=[jax.ShapeDtypeStruct((2, queries[0].shape[2]), F32)] * planes,
        in_specs=[pl.BlockSpec(memory_space=pltpu.SMEM)] + [vmem] * (len(queries) + planes),
        out_specs=[vmem] * planes,
        scratch_shapes=[pltpu.VMEM((2 * planes * shares[0].shape[1], LANES), F32)],
        cost_estimate=pl.CostEstimate(flops=16 * size, bytes_accessed=2 * size, transcendentals=0),
        compiler_params=pltpu.CompilerParams(vmem_limit_bytes=8 * 2**20),
        name="score_shares",
    )(place, *queries, *shares)


def shards(
    attn_in,
    v_grad,
    mlp_hidden,
    out_grad,
    proj_in_attn,
    proj_out_value,
    proj_in_mlp,
    proj_out_mlp,
    query_features,
):
    rank = proj_in_attn.shape[0]
    length = attn_in.shape[1]
    dp = lax.axis_size("dp")
    width = lax.axis_size("tensor")
    examples = attn_in.shape[0] * dp
    dp_pos = lax.axis_index("dp")
    tp_pos = lax.axis_index("tensor")
    chip, core = tp_pos // 2, tp_pos % 2

    planes, depth = 4, dp // 4

    def along_z(x, turn):
        return lax.ppermute(x, "dp", [(k, k // depth * depth + (k + turn) % depth) for k in range(dp)])

    def along_y(x, turn):
        return lax.ppermute(x, "dp", [(k, (k + turn * depth) % dp) for k in range(dp)])

    distances, queries = [[0]], [query_features[None]]

    def widen():
        reach = depth // 2 ** len(queries)
        queries.append(along_z(jnp.concatenate(queries, axis=0) if len(queries) > 1 else queries[0], reach))
        distances.append([d + reach for group in distances for d in group])

    widen()
    acts = (v_grad, attn_in, out_grad, mlp_hidden)
    weights = (proj_out_value, proj_in_attn, proj_out_mlp, proj_in_mlp)
    place = jnp.stack([chip, core, dp_pos, tp_pos]).astype(jnp.int32)
    theirs, own = project(place, acts, weights)
    theirs, own, queries[1] = lax.optimization_barrier((theirs, own, queries[1]))
    other = lax.ppermute(theirs, "tensor", [(k, k ^ 1) for k in range(width)])
    kept, *sent = add_cores(own, other)
    widen()
    parts = [kept] + [
        lax.ppermute(sent[s - 1], "tensor", [(k, (k + 2 * s) % width) for k in range(width)]) for s in (1, 2, 3)
    ]
    parts[2], queries[2] = lax.optimization_barrier((parts[2], queries[2]))
    widen()
    partial = outer(parts, rank, width)
    sums = lax.all_to_all(partial, "tensor", 0, 0, tiled=True)
    sums, queries[3] = lax.optimization_barrier((sums, queries[3]))
    send, norms, *shares = features(place, sums, 1.0 / math.sqrt(length), dp, planes)
    shares = [shares[0]] + [along_y(shares[turn], turn) for turn in range(1, planes)]
    got = lax.all_to_all(send, "dp", 0, 0, tiled=True)
    scored = list(score_shares(place, queries, distances, shares))
    scored[0], got = lax.optimization_barrier((scored[0], got))
    fisher = fisher_block(place, got, examples)
    scored = [scored[0]] + [along_y(scored[turn], -turn) for turn in range(1, planes)]
    scores = sum(scored) / norms
    return (fisher, scores)


def solution(mesh):
    return jax.shard_map(
        shards,
        mesh=mesh,
        in_specs=(
            P("dp", None, "tensor"),
            P("dp", None, "tensor"),
            P("dp", None, "tensor"),
            P("dp", None, "tensor"),
            P(None, "tensor"),
            P(None, "tensor"),
            P(None, "tensor"),
            P(None, "tensor"),
            P(None, "tensor", "dp"),
        ),
        out_specs=(P("dp", None, "tensor"), P("dp", "tensor")),
        check_vma=False,
    )
```

```python
import functools
import math

import jax
import jax.numpy as jnp
from jax import lax
from jax.experimental import pallas as pl
from jax.experimental.pallas import tpu as pltpu
from jax.sharding import PartitionSpec as P

F32 = jnp.float32
BF16 = jnp.bfloat16
LANES = 128
VMEM = pltpu.VMEM
NT = (((1,), (1,)), ((), ()))
TN = (((0,), (0,)), ((), ()))


def dot(a, b, dims):
    return lax.dot_general(a, b, dims, preferred_element_type=F32)


def project_kernel(place, v, a, g, m, wv, wa, wg, wm, theirs_ref, own_ref, value, down, value_weights, down_weights, sems, weight_sems):
    arrays, buffers = (v, a, g, m), (value, value, down, down)
    weights, weight_buffers = (wv, wa, wg, wm), (value_weights, value_weights, down_weights, down_weights)
    half = v.shape[1] // 2
    rank = wv.shape[0]
    chip, core = place[0], place[1]

    def columns(i):
        return pl.ds(0, arrays[i].shape[2]) if i % 2 == 0 else pl.ds(arrays[i - 1].shape[2], arrays[i].shape[2])

    def weight_copy(i):
        target = weight_buffers[i].at[pl.ds(i % 2 * rank, rank), columns(i)]
        return pltpu.make_async_copy(weights[i], target, weight_sems.at[i])

    def copy(i, chunk):
        which = lax.rem(core + 1 + chunk // 2, 2)
        start = pl.multiple_of(which * half, half)
        target = buffers[i].at[chunk, :, columns(i)]
        return pltpu.make_async_copy(arrays[i].at[chunk % 2, pl.ds(start, half)], target, sems.at[chunk, i])

    for i in range(4):
        weight_copy(i).start()
    for chunk in range(2):
        for i in range(4):
            copy(i, chunk).start()
    for i in range(4):
        weight_buffers[i][pl.ds((1 - i % 2) * rank, rank), columns(i)] = jnp.zeros((rank, arrays[i].shape[2]), BF16)
    for i in range(4):
        weight_copy(i).wait()

    def work(out_ref, chunk, carry):
        for i in range(4):
            copy(i, chunk).wait()

        @pl.when(chunk < 2)
        def _():
            for i in range(4):
                copy(i, chunk + 2).start()

        for p, (inputs, matrix) in enumerate(((value, value_weights), (down, down_weights))):
            slot = lax.rem(2 * lax.rem(chunk, 2) + p + 4 - chip, 4)
            out_ref[slot] = dot(inputs[chunk], matrix[...], NT)
        return carry

    lax.fori_loop(0, 2, functools.partial(work, theirs_ref), 0)
    lax.fori_loop(2, 4, functools.partial(work, own_ref), 0)


def project(place, acts, weights):
    sequences, length, _ = acts[0].shape
    half = length // 2
    rank = weights[0].shape[0]
    hbm = pl.BlockSpec(memory_space=pltpu.HBM)
    flops = 2 * sequences * length * sum(w.size for w in weights)
    held_apart = [pltpu.with_memory_space_constraint(x, pltpu.HBM) for x in (*acts, *weights)]
    widths = [acts[0].shape[2] + acts[1].shape[2], acts[2].shape[2] + acts[3].shape[2]]
    return pl.pallas_call(
        project_kernel,
        out_shape=[pltpu.VMEM((4, half, LANES), F32)] * 2,
        in_specs=[pl.BlockSpec(memory_space=pltpu.SMEM)] + [hbm] * 8,
        out_specs=[pl.BlockSpec(memory_space=VMEM)] * 2,
        scratch_shapes=[pltpu.VMEM((4, half, width), BF16) for width in widths]
        + [pltpu.VMEM((2 * rank, width), BF16) for width in widths]
        + [pltpu.SemaphoreType.DMA((4, 4)), pltpu.SemaphoreType.DMA((4,))],
        cost_estimate=pl.CostEstimate(flops=flops, bytes_accessed=2 * sum(a.size for a in acts), transcendentals=0),
        compiler_params=pltpu.CompilerParams(vmem_limit_bytes=32 * 2**20),
        name="project",
    )(place, *held_apart)


def add_kernel(own_ref, other_ref, *out_refs):
    for slot, out_ref in enumerate(out_refs):
        out_ref[...] = own_ref[slot] + other_ref[slot]


def add_cores(own, other):
    return pl.pallas_call(
        add_kernel,
        out_shape=[jax.ShapeDtypeStruct(own.shape[1:], F32)] * 4,
        in_specs=[pl.BlockSpec(memory_space=VMEM)] * 2,
        out_specs=[pl.BlockSpec(memory_space=VMEM)] * 4,
        cost_estimate=pl.CostEstimate(flops=own.size, bytes_accessed=12 * own.size, transcendentals=0),
        compiler_params=pltpu.CompilerParams(vmem_limit_bytes=8 * 2**20),
        name="add_cores",
    )(own, other)


def outer_kernel(rank, a_ref, b_ref, c_ref, d_ref, out_ref, held):
    vectors = ((a_ref[...] + b_ref[...]) + (c_ref[...] + d_ref[...])).astype(BF16)
    held[...] = dot(vectors[:, 0:rank], vectors, TN)
    even = held[pl.ds(0, rank // 2, stride=2), :]
    odd = held[pl.ds(1, rank // 2, stride=2), :]
    lane = lax.broadcasted_iota(jnp.int32, even.shape, 1)
    rows = jnp.where(lane < rank, pltpu.roll(even, rank, 1), odd)
    for target in range(out_ref.shape[0]):
        out_ref[target] = rows


def outer(parts, rank, width):
    return pl.pallas_call(
        functools.partial(outer_kernel, rank),
        out_shape=pltpu.VMEM((width, rank // 2, LANES), F32),
        in_specs=[pl.BlockSpec(memory_space=VMEM)] * 4,
        out_specs=pl.BlockSpec(memory_space=VMEM),
        scratch_shapes=[pltpu.VMEM((rank, LANES), F32)],
        compiler_params=pltpu.CompilerParams(vmem_limit_bytes=8 * 2**20),
        name="outer",
    )(*parts)


def features_kernel(scale, place, sums_ref, send_ref, norm_ref, *share_refs):
    *share_refs, feat_ref = share_refs
    blocks = send_ref.shape[0]
    feats = {}
    squares = {}
    for e in range(2):
        for p in range(2):
            chip = 2 * e + p
            rounded = ((sums_ref[2 * chip] + sums_ref[2 * chip + 1]) * scale).astype(BF16)
            wide = rounded.astype(F32)
            feats[e, p] = wide
            feat_ref[e, p] = wide
            squares[e, p] = jnp.sum(jnp.sum(wide * wide, axis=1, keepdims=True), axis=0, keepdims=True)
    for e in range(2):
        mean = (squares[e, 0] + squares[e, 1]) / (2.0 * blocks * LANES)
        norm_ref[e : e + 1, :] = jnp.broadcast_to(jnp.sqrt(mean + 1e-06), (1, LANES))
    planes = len(share_refs)
    depth = blocks // planes
    for turn, share_ref in enumerate(share_refs):
        start = pl.multiple_of(lax.rem(place[2] // depth + turn, planes) * depth, depth)
        for e in range(2):
            for p in range(2):
                share_ref[e, p * depth : (p + 1) * depth, :] = feat_ref[e, p, pl.ds(start, depth), :]
    row = lax.broadcasted_iota(jnp.int32, (16, LANES), 0)
    for p in range(2):
        total = squares[0, p] + squares[1, p]
        high = total.astype(BF16).astype(F32)
        middle = (total - high).astype(BF16).astype(F32)
        low = total - high - middle
        base = jnp.zeros((16, LANES), F32)
        for e in range(2):
            for k in range(4):
                at = place[3] * 4 + k
                base = jnp.where(row == 5 * e + 1 + k, rounded_row(sums_ref, scale, 2 * e + p, at), base)
        for k, term in enumerate((high, middle, low)):
            base = jnp.where(row == 10 + k, term, base)
        for i in range(blocks):
            tile = jnp.where(row == 0, feats[0, p][i : i + 1, :], base)
            tile = jnp.where(row == 5, feats[1, p][i : i + 1, :], tile)
            send_ref[i, p] = tile.astype(BF16)


def rounded_row(sums_ref, scale, chip, at):
    summed = sums_ref[2 * chip, pl.ds(at, 1), :] + sums_ref[2 * chip + 1, pl.ds(at, 1), :]
    return (summed * scale).astype(BF16).astype(F32)


def features(place, sums, scale, dp, planes):
    blocks = sums.shape[1]
    return pl.pallas_call(
        functools.partial(features_kernel, scale),
        out_shape=[
            pltpu.VMEM((dp, 2, 16, LANES), BF16),
            pltpu.VMEM((2, LANES), F32),
        ]
        + [pltpu.VMEM((2, 2 * blocks // planes, LANES), F32)] * planes,
        in_specs=[pl.BlockSpec(memory_space=pltpu.SMEM), pl.BlockSpec(memory_space=VMEM)],
        out_specs=[pl.BlockSpec(memory_space=VMEM)] * (2 + planes),
        scratch_shapes=[pltpu.VMEM((2, 2, blocks, LANES), F32)],
        compiler_params=pltpu.CompilerParams(vmem_limit_bytes=8 * 2**20),
        name="features",
    )(place, sums)


def fisher_kernel(examples, place, got_ref, out_ref, held):
    sources = got_ref.shape[0]
    count = examples * 32 * LANES
    row = lax.broadcasted_iota(jnp.int32, (LANES, LANES), 0)
    lane = lax.broadcasted_iota(jnp.int32, (LANES, LANES), 1)
    for p in range(2):
        held[...] = got_ref[:, p].astype(F32).reshape(sources * 16, LANES)

        def pick(r):
            return held[pl.ds(r, sources, stride=16), :]

        mine = jnp.concatenate([pick(0), pick(5)], axis=0).astype(BF16)
        theirs = [jnp.concatenate([pick(1 + k), pick(6 + k)], axis=0) for k in range(4)]
        total = jnp.sum(pick(10) + pick(11) + pick(12), axis=0, keepdims=True)
        damping = 0.5 * total / count
        blocks = dot(mine, jnp.concatenate(theirs, axis=1).astype(BF16), TN) * (1.0 / examples)
        for k in range(4):
            on = jnp.logical_and(row == lane, place[2] - 4 * place[3] == k)
            made = blocks[:, k * LANES : (k + 1) * LANES] + jnp.where(on, damping, 0.0)
            out_ref[pl.ds(2 * k + p, LANES, stride=8), :] = made


def fisher_block(place, got, examples):
    made = pl.pallas_call(
        functools.partial(fisher_kernel, examples),
        out_shape=jax.ShapeDtypeStruct((8 * LANES, LANES), F32),
        in_specs=[pl.BlockSpec(memory_space=pltpu.SMEM), pl.BlockSpec(memory_space=VMEM)],
        out_specs=pl.BlockSpec(memory_space=VMEM),
        scratch_shapes=[pltpu.VMEM((got.shape[0] * 16, LANES), F32)],
        compiler_params=pltpu.CompilerParams(vmem_limit_bytes=8 * 2**20),
        name="fisher",
    )(place, got)
    return made.reshape(LANES, 4, 2, LANES).transpose(0, 2, 1, 3).reshape(LANES, 2, 4 * LANES)


def scores_kernel(distances, place, *refs):
    queries = len(distances)
    query_refs, refs = refs[:queries], refs[queries:]
    planes = (len(refs) - 1) // 2
    share_refs, out_refs, held = refs[:planes], refs[planes:-1], refs[-1]
    depth = sum(len(d) for d in distances)
    z = lax.rem(place[2], depth)
    rows = 2 * depth
    for turn, share_ref in enumerate(share_refs):
        for e in range(2):
            held[(2 * turn + e) * rows : (2 * turn + e + 1) * rows, :] = share_ref[e]
    total = None
    for query_ref, group in zip(query_refs, distances):
        for at, distance in enumerate(group):
            source = lax.rem(z + depth - distance, depth)
            vectors = [held[pl.ds(p * depth + source, 2 * planes, stride=rows), :] for p in range(2)]
            wanted = [query_ref[at, p] for p in range(2)]
            part = dot(jnp.concatenate(vectors, axis=1).astype(BF16), jnp.concatenate(wanted, axis=1), NT)
            total = part if total is None else total + part
    for turn, out_ref in enumerate(out_refs):
        out_ref[...] = total[2 * turn : 2 * turn + 2, :]


def score_shares(place, queries, distances, shares):
    planes = len(shares)
    vmem = pl.BlockSpec(memory_space=VMEM)
    size = sum(q.size for q in queries)
    return pl.pallas_call(
        functools.partial(scores_kernel, distances),
        out_shape=[jax.ShapeDtypeStruct((2, queries[0].shape[2]), F32)] * planes,
        in_specs=[pl.BlockSpec(memory_space=pltpu.SMEM)] + [vmem] * (len(queries) + planes),
        out_specs=[vmem] * planes,
        scratch_shapes=[pltpu.VMEM((2 * planes * shares[0].shape[1], LANES), F32)],
        cost_estimate=pl.CostEstimate(flops=16 * size, bytes_accessed=2 * size, transcendentals=0),
        compiler_params=pltpu.CompilerParams(vmem_limit_bytes=8 * 2**20),
        name="score_shares",
    )(place, *queries, *shares)


def shards(
    attn_in,
    v_grad,
    mlp_hidden,
    out_grad,
    proj_in_attn,
    proj_out_value,
    proj_in_mlp,
    proj_out_mlp,
    query_features,
):
    rank = proj_in_attn.shape[0]
    length = attn_in.shape[1]
    dp = lax.axis_size("dp")
    width = lax.axis_size("tensor")
    examples = attn_in.shape[0] * dp
    dp_pos = lax.axis_index("dp")
    tp_pos = lax.axis_index("tensor")
    chip, core = tp_pos // 2, tp_pos % 2

    planes, depth = 4, dp // 4

    def along_z(x, turn):
        return lax.ppermute(x, "dp", [(k, k // depth * depth + (k + turn) % depth) for k in range(dp)])

    def along_y(x, turn):
        return lax.ppermute(x, "dp", [(k, (k + turn * depth) % dp) for k in range(dp)])

    own_queries = query_features[None]
    opposite = along_z(own_queries, depth // 2)

    acts = (v_grad, attn_in, out_grad, mlp_hidden)
    weights = (proj_out_value, proj_in_attn, proj_out_mlp, proj_in_mlp)
    place = jnp.stack([chip, core, dp_pos, tp_pos]).astype(jnp.int32)
    theirs, own = project(place, acts, weights)
    theirs, own, opposite = lax.optimization_barrier((theirs, own, opposite))
    other = lax.ppermute(theirs, "tensor", [(k, k ^ 1) for k in range(width)])
    kept, *sent = add_cores(own, other)
    kept, opposite = lax.optimization_barrier((kept, opposite))
    pair = jnp.concatenate([own_queries, opposite], axis=0)
    turns = (0, 1, 2, -1)
    queries = [along_z(pair, turn) if turn else pair for turn in turns]
    distances = [[turn % depth, (turn + depth // 2) % depth] for turn in turns]
    parts = [kept] + [
        lax.ppermute(sent[s - 1], "tensor", [(k, (k + 2 * s) % width) for k in range(width)]) for s in (1, 2, 3)
    ]
    partial = outer(parts, rank, width)
    sums = lax.all_to_all(partial, "tensor", 0, 0, tiled=True)
    send, norms, *shares = features(place, sums, 1.0 / math.sqrt(length), dp, planes)
    send, *queries = lax.optimization_barrier((send, *queries))
    shares = [shares[0]] + [along_y(shares[turn], turn) for turn in range(1, planes)]
    got = lax.all_to_all(send, "dp", 0, 0, tiled=True)
    scored = list(score_shares(place, queries, distances, shares))
    scored[0], got = lax.optimization_barrier((scored[0], got))
    fisher = fisher_block(place, got, examples)
    scored = [scored[0]] + [along_y(scored[turn], -turn) for turn in range(1, planes)]
    scores = sum(scored) / norms
    return (fisher, scores)


def solution(mesh):
    return jax.shard_map(
        shards,
        mesh=mesh,
        in_specs=(
            P("dp", None, "tensor"),
            P("dp", None, "tensor"),
            P("dp", None, "tensor"),
            P("dp", None, "tensor"),
            P(None, "tensor"),
            P(None, "tensor"),
            P(None, "tensor"),
            P(None, "tensor"),
            P(None, "tensor", "dp"),
        ),
        out_specs=(P("dp", None, "tensor"), P("dp", "tensor")),
        check_vma=False,
    )
```
